512 devices in a mesh: ctx: 64 (over x, z, y_hi), ch: 8 (over y_lo, core).
Axes of the slice: x: 4, y: 8 (y_hi: 2, y_lo: 4; y = y_hi * 4 + y_lo), z: 8, core: 2. Of those that a mesh axis runs over, the one named last changes fastest.
Arguments:
- outer_gate: bfloat16 [8192, 4096], P('ctx', 'ch'), may hold values from -6 to 6
- inner_gate: bfloat16 [8192, 4096], P('ctx', 'ch'), may hold values from -6 to 6
- value_path: bfloat16 [8192, 4096], P('ctx', 'ch'), may hold values from -6 to 6
- long_filter: float32 [8192, 4096], P('ctx', 'ch'), may hold values from -0.0625 to 0.0625
- skip_gain: float32 [4096], P('ch'), may hold values from 0.25 to 1.75
- cotangent: bfloat16 [8192, 4096], P('ctx', 'ch'), may hold values from -32 to 32
Outputs:
- hyena_out: bfloat16 [8192, 4096], P('ctx', 'ch')
- grad_outer: bfloat16 [8192, 4096], P('ctx', 'ch')
- grad_inner: bfloat16 [8192, 4096], P('ctx', 'ch')
- grad_value: bfloat16 [8192, 4096], P('ctx', 'ch')
- grad_filter: float32 [8192, 4096], P('ctx', 'ch')
The draws below stay inside these ranges and needn't reach their ends.
All inputs are finite; a program needn't handle non-finite values.
Results may differ from the reference program's by a relative error of at most 0.001.
Values may be sent and summed in bfloat16 or wider, within the bound.
A program may use at most 64 MiB of HBM per device.

```python
import math
import jax
import jax.numpy as jnp
from jax import lax

CH_DEV = 512
SEQ = 8192
CHANNELS = 4096


def draw_cotangent(key, part):
    key = jax.random.fold_in(key, 7)
    key_noise, key_scale = jax.random.split(key, 2)
    position = (lax_free_index(CHANNELS) % CH_DEV).astype(jnp.float32) / CH_DEV
    channel_scale = jnp.exp(jax.random.uniform(key_scale, (CHANNELS,), jnp.float32, math.log(1.5), math.log(3.0))) * jnp.exp(math.log(3.0) * position)
    noise = jnp.clip(jax.random.normal(key_noise, (SEQ, CHANNELS), jnp.float32), -3.5, 3.5)
    values = channel_scale[None, :] * noise
    return values.astype(jnp.bfloat16)


def lax_free_index(count):
    return jnp.arange(count, dtype=jnp.int32)


def steps_of(key, dims, shards, low, high):
    gain, own = 1.0, jax.random.fold_in(key, 6)
    for dim, blocks in shards:
        draws = jnp.exp(jax.random.uniform(jax.random.fold_in(own, dim), (blocks,), jnp.float32, low / len(shards), high / len(shards)))
        gain = gain * jnp.repeat(draws, dims[dim] // blocks).reshape([-1 if axis == dim else 1 for axis in range(len(dims))])
    return gain


def scatter_about(rng, dims, deviation, most, cuts=(), kind=jnp.bfloat16):
    entries = deviation * jax.random.normal(rng, dims, jnp.float32)
    if cuts:
        entries = entries * steps_of(rng, dims, cuts, -0.22, 0.18)
    return jnp.clip(entries, -most, most).astype(kind)


def setup_inputs(seed: int = 0) -> dict:
    arg_keys = jax.random.split(jax.random.key(seed), 7)
    return {
        "outer_gate": scatter_about(arg_keys[0], (SEQ, CHANNELS), 1.0, 6.0, ((0, 64), (1, 8))),
        "inner_gate": scatter_about(arg_keys[1], (SEQ, CHANNELS), 1.0, 6.0, ((0, 64), (1, 8))),
        "value_path": scatter_about(arg_keys[2], (SEQ, CHANNELS), 1.0, 6.0, ((0, 64), (1, 8))),
        "long_filter": scatter_about(arg_keys[3], (SEQ, CHANNELS), SEQ ** -0.5, 0.0625, ((0, 64), (1, 8)), jnp.float32),
        "skip_gain": jnp.clip(1.0 + 0.15 * jax.random.normal(arg_keys[4], (CHANNELS,), jnp.float32), 0.25, 1.75),
        "cotangent": draw_cotangent(jax.random.fold_in(arg_keys[6], 71), 0),
    }


def causal_block(operands):
    taps, mixed, grad_conv = operands
    length = taps.shape[0]
    padded = 2 * length
    filter_spec = jnp.fft.fft(taps, n=padded, axis=0)
    mixed_spec = jnp.fft.fft(mixed, n=padded, axis=0)
    grad_spec = jnp.fft.fft(grad_conv, n=padded, axis=0)
    convolved = jnp.fft.ifft(filter_spec * mixed_spec, axis=0)[:length].real
    back_mixed = jnp.fft.ifft(jnp.conj(filter_spec) * grad_spec, axis=0)[:length].real
    lag_grad = jnp.fft.ifft(jnp.conj(mixed_spec) * grad_spec, axis=0)[:length].real
    return (convolved.astype(jnp.float32), back_mixed.astype(jnp.float32), lag_grad.astype(jnp.float32))

def reference(outer_gate, inner_gate, value_path, long_filter, skip_gain, cotangent):
    mixed = inner_gate.astype(jnp.float32) * value_path.astype(jnp.float32)
    grad_conv = cotangent.astype(jnp.float32) * outer_gate.astype(jnp.float32)
    block = math.gcd(CHANNELS, 256)

    def split_block(array):
        return array.reshape(SEQ, CHANNELS // block, block).transpose(1, 0, 2)

    def join_block(array):
        return array.transpose(1, 0, 2).reshape(SEQ, CHANNELS)
    results = lax.map(causal_block, (split_block(long_filter.astype(jnp.float32)), split_block(mixed), split_block(grad_conv)))
    convolved = join_block(results[0])
    back_mixed = join_block(results[1])
    lag_grad = join_block(results[2])
    gated_base = convolved + skip_gain[None, :] * mixed
    hyena_out = (outer_gate.astype(jnp.float32) * gated_base).astype(jnp.bfloat16)
    grad_outer = (cotangent.astype(jnp.float32) * gated_base).astype(jnp.bfloat16)
    grad_mixed = back_mixed + skip_gain[None, :] * grad_conv
    grad_inner = (grad_mixed * value_path.astype(jnp.float32)).astype(jnp.bfloat16)
    grad_value = (grad_mixed * inner_gate.astype(jnp.float32)).astype(jnp.bfloat16)
    squares = jnp.sum(lag_grad * lag_grad)
    limit = SEQ * math.sqrt(CHANNELS)
    grad_filter = lag_grad * jnp.minimum(1.0, limit / jnp.sqrt(squares + 1e-06))
    return (hyena_out, grad_outer, grad_inner, grad_value, grad_filter)
```

```python
import functools

import jax
import jax.numpy as jnp
import numpy as np
from jax import lax
from jax.experimental import pallas as pl
from jax.experimental.pallas import tpu as pltpu
from jax.sharding import PartitionSpec as P

F32 = jnp.float32
BF16 = jnp.bfloat16
MESH = pl.DeviceIdType.MESH

NCTX = 64
NCH = 8
BLK = 128
LANES = 512
NAR = LANES // NCTX
ROWS = 3 * NAR


def split(x):
    hi = x.astype(BF16)
    lo = (x - hi.astype(F32)).astype(BF16)
    return hi, lo


def tables():
    total = NCTX * BLK
    p = np.arange(NCTX)
    s = np.arange(BLK)
    k = np.arange(NCTX) + 0.25
    a1 = 2 * np.pi * np.outer(k, p) / NCTX
    w1 = np.concatenate([np.cos(a1), -np.sin(a1)], axis=0)
    at = 2 * np.pi * np.outer(k, s) / total
    tw = np.stack([np.cos(at), -np.sin(at)])
    a2 = 2 * np.pi * (np.outer(s, s) % BLK) / BLK
    c, sn = np.cos(a2), np.sin(a2)
    w2 = np.block([[c, -sn], [sn, c]])

    def parts(m):
        hi = m.astype(BF16)
        lo = (m - hi.astype(np.float64)).astype(BF16)
        return hi, lo

    w1h, w1l = parts(w1)
    w1f = np.concatenate([w1h, w1l, w1h], axis=1)
    w1i = np.concatenate([w1h.T, w1l.T, w1h.T], axis=1)
    w2h, w2l = parts(w2)
    w2f = np.stack([w2h, w2l])
    w2i = np.stack([w2h.T, w2l.T])
    return w1f, w1i, tw.astype(np.float32), w2f, w2i


def dot(a, b):
    return jnp.dot(a, b, preferred_element_type=F32)


def dot3(x, w_ref):
    hi, lo = split(x)
    wh = w_ref[0]
    return dot(hi, wh) + (dot(hi, w_ref[1]) + dot(lo, wh))


def conv_kernel(
    outer, inner, value, cot, filt, w1f, w1i, tw, w2f, w2i,
    back, sums,
    send, recv, ret, part, chbuf,
    send_sem, recv_sem, send2_sem, recv2_sem, sq_send, sq_recv, loc_sem, sqx_send, sqx_recv,
):
    me = lax.axis_index("ctx")
    ch = lax.axis_index("ch")

    barrier = pltpu.get_barrier_semaphore()

    def greet(i, _):
        pl.semaphore_signal(
            barrier, inc=1, device_id={"ctx": lax.rem(me + i, NCTX)}, device_id_type=MESH
        )
        return 0

    lax.fori_loop(1, NCTX, greet, 0)
    for j in range(1, NCH):
        pl.semaphore_signal(
            barrier, inc=1, device_id={"ch": lax.rem(ch + j, NCH)}, device_id_type=MESH
        )

    mixed = inner[...].astype(F32) * value[...].astype(F32)
    send[:, 0:NAR, :] = mixed.T.reshape(NCTX, NAR, BLK)
    gconv = cot[...].astype(F32) * outer[...].astype(F32)
    send[:, NAR : 2 * NAR, :] = gconv.T.reshape(NCTX, NAR, BLK)
    send[:, 2 * NAR : 3 * NAR, :] = filt[...].T.reshape(NCTX, NAR, BLK)

    pl.semaphore_wait(barrier, NCTX - 1 + NCH - 1)

    own = pltpu.make_async_copy(send.at[me], recv.at[pl.ds(me * ROWS, ROWS)], recv_sem)
    own.start()

    def scatter(i, _):
        to = lax.rem(me + i, NCTX)
        pltpu.make_async_remote_copy(
            src_ref=send.at[to],
            dst_ref=recv.at[pl.ds(me * ROWS, ROWS)],
            send_sem=send_sem,
            recv_sem=recv_sem,
            device_id={"ctx": to},
            device_id_type=MESH,
        ).start()
        return 0

    lax.fori_loop(1, NCTX, scatter, 0)
    pltpu.make_async_copy(recv, recv, recv_sem).wait()

    tr, ti = tw[0], tw[1]
    wa, wb = w1f[...], w1i[...]

    def forward(sig, c):
        x = recv[pl.ds(sig * NAR + c, NCTX, stride=ROWS), :]
        hi, lo = split(x)
        z = dot(wa, jnp.concatenate([hi, hi, lo], axis=0))
        zr, zi = z[:NCTX], z[NCTX:]
        return jnp.concatenate([zr * tr - zi * ti, zr * ti + zi * tr], axis=1)

    def inverse(v):
        vr, vi = v[:, :BLK], v[:, BLK:]
        u = jnp.concatenate([vr * tr + vi * ti, vi * tr - vr * ti], axis=0)
        hi, lo = split(u)
        return dot(wb, jnp.concatenate([hi, hi, lo], axis=0)) * (1.0 / (NCTX * BLK))

    def channel(c, acc):
        u = jnp.concatenate([forward(0, c), forward(1, c), forward(2, c)], axis=0)
        x = dot3(u, w2f)
        m, g, f = x[:NCTX], x[NCTX : 2 * NCTX], x[2 * NCTX :]
        mr, mi = m[:, :BLK], m[:, BLK:]
        gr, gi = g[:, :BLK], g[:, BLK:]
        fr, fi = f[:, :BLK], f[:, BLK:]
        y = jnp.concatenate(
            [
                jnp.concatenate([fr * mr - fi * mi, fr * mi + fi * mr], axis=1),
                jnp.concatenate([fr * gr + fi * gi, fr * gi - fi * gr], axis=1),
                jnp.concatenate([mr * gr + mi * gi, mr * gi - mi * gr], axis=1),
            ],
            axis=0,
        )
        v = dot3(y, w2i)
        ret[pl.ds(c, NCTX, stride=ROWS), :] = inverse(v[:NCTX])
        ret[pl.ds(NAR + c, NCTX, stride=ROWS), :] = inverse(v[NCTX : 2 * NCTX])
        lag = inverse(v[2 * NCTX :])
        ret[pl.ds(2 * NAR + c, NCTX, stride=ROWS), :] = lag
        sq = lag * lag
        return acc + jnp.sum(sq.reshape(NCTX // 8, 8, BLK), axis=0)

    acc = lax.fori_loop(0, NAR, channel, jnp.zeros((8, BLK), F32))

    part[...] = acc
    chbuf[ch] = acc
    for j in range(1, NCH):
        pltpu.make_async_remote_copy(
            src_ref=part,
            dst_ref=chbuf.at[ch],
            send_sem=sq_send,
            recv_sem=sq_recv,
            device_id={"ch": lax.rem(ch + j, NCH)},
            device_id_type=MESH,
        ).start()

    own2 = pltpu.make_async_copy(ret.at[pl.ds(me * ROWS, ROWS)], back.at[me], recv2_sem)
    own2.start()

    def gather(i, _):
        to = lax.rem(me + i, NCTX)
        pltpu.make_async_remote_copy(
            src_ref=ret.at[pl.ds(to * ROWS, ROWS)],
            dst_ref=back.at[me],
            send_sem=send2_sem,
            recv_sem=recv2_sem,
            device_id={"ctx": to},
            device_id_type=MESH,
        ).start()
        return 0

    lax.fori_loop(1, NCTX, gather, 0)

    pltpu.make_async_copy(chbuf.at[pl.ds(0, NCH - 1)], chbuf.at[pl.ds(0, NCH - 1)], sq_send).wait()
    pltpu.make_async_copy(chbuf.at[pl.ds(0, NCH - 1)], chbuf.at[pl.ds(0, NCH - 1)], sq_recv).wait()
    group = jnp.sum(jnp.sum(chbuf[...], axis=0), axis=0, keepdims=True)
    part[0:1, :] = group
    sums[me] = group

    def spread(i, _):
        to = lax.rem(me + i, NCTX)
        pltpu.make_async_remote_copy(
            src_ref=part.at[pl.ds(0, 1)],
            dst_ref=sums.at[me],
            send_sem=sqx_send,
            recv_sem=sqx_recv,
            device_id={"ctx": to},
            device_id_type=MESH,
        ).start()
        return 0

    lax.fori_loop(1, NCTX, spread, 0)

    rest = pl.ds(0, (NCTX - 1) * ROWS)
    pltpu.make_async_copy(recv.at[rest], recv.at[rest], send_sem).wait()
    pltpu.make_async_copy(ret.at[rest], ret.at[rest], send2_sem).wait()
    others = pl.ds(0, NCTX - 1)
    pltpu.make_async_copy(sums.at[others], sums.at[others], sqx_send).wait()
    pltpu.make_async_copy(sums.at[others], sums.at[others], sqx_recv).wait()
    pltpu.make_async_copy(back, back, recv2_sem).wait()


def gate_kernel(
    outer, inner, value, cot, skip, back, sums, hyena, gouter, ginner, gvalue, gfilter
):
    inner_f = inner[...].astype(F32)
    value_f = value[...].astype(F32)
    outer_f = outer[...].astype(F32)
    cot_f = cot[...].astype(F32)
    gain = skip[...]
    conv = back[:, 0:NAR, :].reshape(LANES, BLK).T
    base = conv + gain * (inner_f * value_f)
    hyena[...] = (outer_f * base).astype(BF16)
    gouter[...] = (cot_f * base).astype(BF16)
    gmixed = back[:, NAR : 2 * NAR, :].reshape(LANES, BLK).T + gain * (cot_f * outer_f)
    ginner[...] = (gmixed * value_f).astype(BF16)
    gvalue[...] = (gmixed * inner_f).astype(BF16)
    squares = jnp.sum(jnp.sum(sums[...], axis=0), axis=1, keepdims=True)
    limit = float(NCTX * BLK) * float(np.sqrt(LANES * NCH))
    scale = jnp.minimum(1.0, limit / jnp.sqrt(squares + 1e-06))
    gfilter[...] = back[:, 2 * NAR :, :].reshape(LANES, BLK).T * scale


def local(outer_gate, inner_gate, value_path, long_filter, skip_gain, cotangent):
    vmem = pl.BlockSpec(memory_space=pltpu.VMEM)
    consts = tables()
    back, sums = pl.pallas_call(
        conv_kernel,
        out_shape=(
            jax.ShapeDtypeStruct((NCTX, ROWS, BLK), F32),
            jax.ShapeDtypeStruct((NCTX, 1, BLK), F32),
        ),
        in_specs=[vmem] * 10,
        out_specs=(vmem, vmem),
        scratch_shapes=[
            pltpu.VMEM((NCTX, ROWS, BLK), F32),
            pltpu.VMEM((NCTX * ROWS, BLK), F32),
            pltpu.VMEM((NCTX * ROWS, BLK), F32),
            pltpu.VMEM((8, BLK), F32),
            pltpu.VMEM((NCH, 8, BLK), F32),
        ]
        + [pltpu.SemaphoreType.DMA] * 9,
        compiler_params=pltpu.CompilerParams(
            collective_id=0, has_side_effects=True, vmem_limit_bytes=32 * 1024 * 1024
        ),
    )(outer_gate, inner_gate, value_path, cotangent, long_filter, *consts)
    arr = jax.ShapeDtypeStruct((BLK, LANES), BF16)
    return pl.pallas_call(
        gate_kernel,
        out_shape=(arr, arr, arr, arr, jax.ShapeDtypeStruct((BLK, LANES), F32)),
        in_specs=[vmem] * 7,
        out_specs=(vmem,) * 5,
        compiler_params=pltpu.CompilerParams(vmem_limit_bytes=32 * 1024 * 1024),
    )(outer_gate, inner_gate, value_path, cotangent, skip_gain.reshape(1, LANES), back, sums)


def solution(mesh):
    big = P("ctx", "ch")
    return jax.shard_map(
        local,
        mesh=mesh,
        in_specs=(big, big, big, big, P("ch"), big),
        out_specs=(big,) * 5,
        check_vma=False,
    )
```

```python
import jax
import jax.numpy as jnp
import numpy as np
from jax import lax
from jax.experimental import pallas as pl
from jax.experimental.pallas import tpu as pltpu
from jax.sharding import PartitionSpec as P

F32 = jnp.float32
BF16 = jnp.bfloat16
MESH = pl.DeviceIdType.MESH

NCTX = 64
NCH = 8
VMEM_LIMIT = 60 * 1024 * 1024
BLK = 128
LANES = 512
NAR = LANES // NCTX


def split(x):
    hi = x.astype(BF16)
    lo = (x - hi.astype(F32)).astype(BF16)
    return hi, lo


def tables():
    total = NCTX * BLK
    p = np.arange(NCTX)
    s = np.arange(BLK)
    k = np.arange(NCTX) + 0.25
    a1 = 2 * np.pi * np.outer(k, p) / NCTX
    w1 = np.concatenate([np.cos(a1), -np.sin(a1)], axis=0)
    at = 2 * np.pi * np.outer(k, s) / total
    tw = np.stack([np.cos(at), -np.sin(at)])
    a2 = 2 * np.pi * (np.outer(s, s) % BLK) / BLK
    c, sn = np.cos(a2), np.sin(a2)
    w2 = np.block([[c, -sn], [sn, c]])

    def parts(m):
        hi = m.astype(BF16)
        lo = (m - hi.astype(np.float64)).astype(BF16)
        return hi, lo

    w1h, w1l = parts(w1)
    w1f = np.concatenate([w1h, w1l, w1h], axis=1)
    w1i = np.concatenate([w1h.T, w1l.T, w1h.T], axis=1)
    w2h, w2l = parts(w2)
    w2f = np.stack([w2h, w2l])
    w2i = np.stack([w2h.T, w2l.T])
    return w1f, w1i, tw.astype(np.float32), w2f, w2i


def dot(a, b):
    return jnp.dot(a, b, preferred_element_type=F32)


def dot3(x, w_ref):
    hi, lo = split(x)
    wh = w_ref[0]
    return dot(hi, wh) + (dot(hi, w_ref[1]) + dot(lo, wh))


def place(me):
    return lax.div(me, 16), lax.rem(lax.div(me, 2), 8), lax.rem(me, 2)


def peer(me, i):
    x, z, y = place(me)
    k, j = lax.div(i, 8), lax.rem(i, 8)
    dy = 1 - lax.div(k, 4)
    k = lax.rem(k, 4)
    dx = 2 + lax.div(k + 1, 2) * (1 - 2 * lax.rem(k, 2))
    dz = 4 + lax.div(j + 1, 2) * (1 - 2 * lax.rem(j, 2))
    return lax.rem(x + dx, 4) * 16 + lax.rem(z + dz, 8) * 2 + lax.rem(y + dy, 2)


def conv_kernel(
    outer_h, inner_h, value_h, cot_h, filt_h, w1f_h, w1i_h, tw_h, w2f_h, w2i_h,
    back, back_lag, total,
    outer, inner, value, cot, filt, w1f, w1i, tw, w2f, w2i,
    send, send_f, recv, recv_f, ret, ret_lag, spec, part, sums,
    load_sem, send_sem, recv_sem, sendf_sem, recvf_sem, sendl_sem, recvl_sem,
    sendr_sem, recvr_sem, sq_send, sq_recv, own_sem,
):
    me = lax.axis_index("ctx")
    ch = lax.axis_index("ch")
    x, z, y = place(me)

    loads = [
        pltpu.make_async_copy(src, dst, load_sem.at[n])
        for n, (src, dst) in enumerate(
            [
                (inner_h, inner), (value_h, value), (cot_h, cot), (outer_h, outer),
                (filt_h, filt), (w1f_h, w1f), (w1i_h, w1i), (tw_h, tw), (w2f_h, w2f),
                (w2i_h, w2i),
            ]
        )
    ]
    for load in loads:
        load.start()

    barrier = pltpu.get_barrier_semaphore()

    def greet(i, _):
        pl.semaphore_signal(
            barrier, inc=1, device_id={"ctx": peer(me, i)}, device_id_type=MESH
        )
        return 0

    lax.fori_loop(0, NCTX - 1, greet, 0)
    for j in range(1, NCH):
        pl.semaphore_signal(
            barrier, inc=1, device_id={"ch": lax.rem(ch + j, NCH)}, device_id_type=MESH
        )

    for load in loads[:5]:
        load.wait()
    mixed = inner[...].astype(F32) * value[...].astype(F32)
    send[:, 0:NAR, :] = mixed.T.reshape(NCTX, NAR, BLK)
    gconv = cot[...].astype(F32) * outer[...].astype(F32)
    send[:, NAR : 2 * NAR, :] = gconv.T.reshape(NCTX, NAR, BLK)
    send_f[...] = filt[...].T.reshape(NCTX, NAR, BLK)
    for load in loads[5:]:
        load.wait()

    pl.semaphore_wait(barrier, NCTX - 1 + NCH - 1)

    def spread(src, dst, send_s, recv_s):
        def one(i, _):
            to = peer(me, i)
            pltpu.make_async_remote_copy(
                src_ref=src(to),
                dst_ref=dst(me),
                send_sem=send_s,
                recv_sem=recv_s,
                device_id={"ctx": to},
                device_id_type=MESH,
            ).start()
            return 0

        lax.fori_loop(0, NCTX - 1, one, 0)
        pltpu.make_async_copy(src(me), dst(me), recv_s).start()

    spread(lambda d: send.at[d], lambda d: recv.at[pl.ds(d * 16, 16)], send_sem, recv_sem)
    spread(lambda d: send_f.at[d], lambda d: recv_f.at[pl.ds(d * 8, 8)], sendf_sem, recvf_sem)

    tr, ti = tw[0], tw[1]
    wa, wb = w1f[...], w1i[...]

    def forward(rows):
        hi, lo = split(rows)
        z = dot(wa, jnp.concatenate([hi, hi, lo], axis=0))
        zr, zi = z[:NCTX], z[NCTX:]
        return jnp.concatenate([zr * tr - zi * ti, zr * ti + zi * tr], axis=1)

    def inverse(v):
        vr, vi = v[:, :BLK], v[:, BLK:]
        u = jnp.concatenate([vr * tr + vi * ti, vi * tr - vr * ti], axis=0)
        hi, lo = split(u)
        return dot(wb, jnp.concatenate([hi, hi, lo], axis=0)) * (1.0 / (NCTX * BLK))

    def correlate(a, b):
        ar, ai, br, bi = a[:, :BLK], a[:, BLK:], b[:, :BLK], b[:, BLK:]
        return jnp.concatenate([ar * br + ai * bi, ar * bi - ai * br], axis=1)

    def convolve(a, b):
        ar, ai, br, bi = a[:, :BLK], a[:, BLK:], b[:, :BLK], b[:, BLK:]
        return jnp.concatenate([ar * br - ai * bi, ar * bi + ai * br], axis=1)

    def pieces(v):
        return [v[n * NCTX : (n + 1) * NCTX] for n in range(v.shape[0] // NCTX)]

    def lag_pair(n, acc):
        c = 2 * n
        u = [forward(recv[pl.ds(c + d, NCTX, stride=16), :]) for d in (0, 1, NAR, NAR + 1)]
        f = dot3(jnp.concatenate(u, axis=0), w2f)
        spec[n] = f
        m0, m1, g0, g1 = pieces(f)
        v = dot3(jnp.concatenate([correlate(m0, g0), correlate(m1, g1)], axis=0), w2i)
        for d, part_v in enumerate(pieces(v)):
            lag = inverse(part_v)
            ret_lag[pl.ds(c + d, NCTX, stride=8), :] = lag
            acc = acc + jnp.sum((lag * lag).reshape(NCTX // 8, 8, BLK), axis=0)
        return acc

    def conv_pair(n, carry):
        c = 2 * n
        u = [forward(recv_f[pl.ds(c + d, NCTX, stride=8), :]) for d in (0, 1)]
        f0, f1 = pieces(dot3(jnp.concatenate(u, axis=0), w2f))
        m0, m1, g0, g1 = pieces(spec[n])
        v = dot3(
            jnp.concatenate(
                [convolve(f0, m0), convolve(f1, m1), correlate(f0, g0), correlate(f1, g1)],
                axis=0,
            ),
            w2i,
        )
        for d, part_v in zip((0, 1, NAR, NAR + 1), pieces(v)):
            ret[pl.ds(c + d, NCTX, stride=16), :] = inverse(part_v)
        return carry

    def share(stage, mine, value, device):
        part[stage] = value
        sums[stage, mine] = value
        for j in range(1, 8):
            pltpu.make_async_remote_copy(
                src_ref=part.at[stage],
                dst_ref=sums.at[stage, mine],
                send_sem=sq_send.at[stage],
                recv_sem=sq_recv.at[stage],
                device_id=device(lax.rem(mine + j, 8)),
                device_id_type=MESH,
            ).start()

    def gathered(stage):
        seven = sums.at[stage, pl.ds(0, 7)]
        pltpu.make_async_copy(seven, seven, sq_send.at[stage]).wait()
        pltpu.make_async_copy(seven, seven, sq_recv.at[stage]).wait()
        return jnp.sum(sums[stage], axis=0)

    pltpu.make_async_copy(recv, recv, recv_sem).wait()
    acc = lax.fori_loop(0, NAR // 2, lag_pair, jnp.zeros((8, BLK), F32))
    share(0, ch, acc, lambda k: {"ch": k})
    spread(lambda d: ret_lag.at[pl.ds(d * 8, 8)], lambda d: back_lag.at[d], sendl_sem, recvl_sem)

    pltpu.make_async_copy(recv_f, recv_f, recvf_sem).wait()
    lax.fori_loop(0, 2, conv_pair, 0)
    share(1, z, gathered(0), lambda k: {"ctx": x * 16 + k * 2 + y})
    lax.fori_loop(2, 4, conv_pair, 0)
    share(2, x * 2 + y, gathered(1), lambda k: {"ctx": lax.div(k, 2) * 16 + z * 2 + lax.rem(k, 2)})
    spread(lambda d: ret.at[pl.ds(d * 16, 16)], lambda d: back.at[d], sendr_sem, recvr_sem)
    total[...] = gathered(2)

    others = pl.ds(0, (NCTX - 1) * 16)
    pltpu.make_async_copy(recv.at[others], recv.at[others], send_sem).wait()
    pltpu.make_async_copy(ret.at[others], ret.at[others], sendr_sem).wait()
    others = pl.ds(0, (NCTX - 1) * 8)
    pltpu.make_async_copy(recv_f.at[others], recv_f.at[others], sendf_sem).wait()
    pltpu.make_async_copy(ret_lag.at[others], ret_lag.at[others], sendl_sem).wait()
    pltpu.make_async_copy(back_lag, back_lag, recvl_sem).wait()
    pltpu.make_async_copy(back, back, recvr_sem).wait()


def gate_kernel(
    outer_h, inner_h, value_h, cot_h, skip, back_h, lag_h, total,
    hyena, gouter, ginner, gvalue, gfilter,
    outer, inner, value, cot, back, back_lag, sem,
):
    loads = [
        pltpu.make_async_copy(src, dst, sem.at[n])
        for n, (src, dst) in enumerate(
            [
                (back_h, back), (inner_h, inner), (value_h, value), (outer_h, outer),
                (cot_h, cot), (lag_h, back_lag),
            ]
        )
    ]
    for load in loads:
        load.start()
    for load in loads:
        load.wait()
    inner_f = inner[...].astype(F32)
    value_f = value[...].astype(F32)
    outer_f = outer[...].astype(F32)
    cot_f = cot[...].astype(F32)
    gain = skip[...]
    conv = back[:, 0:NAR, :].reshape(LANES, BLK).T
    base = conv + gain * (inner_f * value_f)
    hyena[...] = (outer_f * base).astype(BF16)
    gouter[...] = (cot_f * base).astype(BF16)
    gmixed = back[:, NAR : 2 * NAR, :].reshape(LANES, BLK).T + gain * (cot_f * outer_f)
    ginner[...] = (gmixed * value_f).astype(BF16)
    gvalue[...] = (gmixed * inner_f).astype(BF16)
    squares = jnp.sum(jnp.sum(total[...], axis=0, keepdims=True), axis=1, keepdims=True)
    limit = float(NCTX * BLK) * float(np.sqrt(LANES * NCH))
    scale = jnp.minimum(1.0, limit / jnp.sqrt(squares + 1e-06))
    gfilter[...] = back_lag[...].reshape(LANES, BLK).T * scale


def local(outer_gate, inner_gate, value_path, long_filter, skip_gain, cotangent):
    vmem = pl.BlockSpec(memory_space=pltpu.VMEM)
    hbm = pl.BlockSpec(memory_space=pltpu.HBM)
    consts = tables()
    dma = pltpu.SemaphoreType.DMA
    back, back_lag, total = pl.pallas_call(
        conv_kernel,
        out_shape=(
            jax.ShapeDtypeStruct((NCTX, 2 * NAR, BLK), F32),
            jax.ShapeDtypeStruct((NCTX, NAR, BLK), F32),
            jax.ShapeDtypeStruct((8, BLK), F32),
        ),
        in_specs=[hbm] * 10,
        out_specs=(hbm, hbm, vmem),
        scratch_shapes=[pltpu.VMEM((BLK, LANES), BF16)] * 4
        + [pltpu.VMEM((BLK, LANES), F32)]
        + [pltpu.VMEM(c.shape, c.dtype) for c in consts]
        + [
            pltpu.VMEM((NCTX, 2 * NAR, BLK), F32),
            pltpu.VMEM((NCTX, NAR, BLK), F32),
            pltpu.VMEM((NCTX * 2 * NAR, BLK), F32),
            pltpu.VMEM((NCTX * NAR, BLK), F32),
            pltpu.VMEM((NCTX * 2 * NAR, BLK), F32),
            pltpu.VMEM((NCTX * NAR, BLK), F32),
            pltpu.VMEM((NAR // 2, 4 * NCTX, 2 * BLK), F32),
            pltpu.VMEM((3, 8, BLK), F32),
            pltpu.VMEM((3, 8, 8, BLK), F32),
            dma((10,)),
        ]
        + [dma] * 8
        + [dma((3,)), dma((3,)), dma],
        compiler_params=pltpu.CompilerParams(
            collective_id=0, has_side_effects=True, vmem_limit_bytes=VMEM_LIMIT
        ),
    )(outer_gate, inner_gate, value_path, cotangent, long_filter, *consts)
    arr = jax.ShapeDtypeStruct((BLK, LANES), BF16)
    return pl.pallas_call(
        gate_kernel,
        out_shape=(arr, arr, arr, arr, jax.ShapeDtypeStruct((BLK, LANES), F32)),
        in_specs=[hbm] * 4 + [vmem, hbm, hbm, vmem],
        out_specs=(vmem,) * 5,
        scratch_shapes=[pltpu.VMEM((BLK, LANES), BF16)] * 4
        + [
            pltpu.VMEM((NCTX, 2 * NAR, BLK), F32),
            pltpu.VMEM((NCTX, NAR, BLK), F32),
            dma((6,)),
        ],
        compiler_params=pltpu.CompilerParams(vmem_limit_bytes=VMEM_LIMIT),
    )(
        outer_gate, inner_gate, value_path, cotangent, skip_gain.reshape(1, LANES),
        back, back_lag, total,
    )


def solution(mesh):
    big = P("ctx", "ch")
    return jax.shard_map(
        local,
        mesh=mesh,
        in_specs=(big, big, big, big, P("ch"), big),
        out_specs=(big,) * 5,
        check_vma=False,
    )
```

```python
import jax
import jax.numpy as jnp
import numpy as np
from jax import lax
from jax.experimental import pallas as pl
from jax.experimental.pallas import tpu as pltpu
from jax.sharding import PartitionSpec as P

F32 = jnp.float32
BF16 = jnp.bfloat16
MESH = pl.DeviceIdType.MESH

NCTX = 64
NCH = 8
VMEM_LIMIT = 60 * 1024 * 1024
BLK = 128
LANES = 512
NAR = LANES // NCTX
HALF = NAR // 2
LN2 = float(np.log(2.0))
DIGITS = 511.0
CODE_MAX = 255.0 * DIGITS + 255.0
STEP = 2.0**-22
TINY = 2.0**-80
FILTER_CODE = (CODE_MAX / 24.0, 28.0)
LAG_CODE = (CODE_MAX / 128.0, 102.0)


def split(x):
    hi = x.astype(BF16)
    lo = (x - hi.astype(F32)).astype(BF16)
    return hi, lo


def tables():
    total = NCTX * BLK
    p = np.arange(NCTX)
    s = np.arange(BLK)
    k = np.arange(NCTX) + 0.25
    a1 = 2 * np.pi * np.outer(k, p) / NCTX
    w1 = np.concatenate([np.cos(a1), -np.sin(a1)], axis=0)
    at = 2 * np.pi * np.outer(k, s) / total
    tw = np.stack([np.cos(at), -np.sin(at)])
    a2 = 2 * np.pi * (np.outer(s, s) % BLK) / BLK
    c, sn = np.cos(a2), np.sin(a2)
    w2 = np.block([[c, -sn], [sn, c]])

    def parts(m):
        hi = m.astype(BF16)
        lo = (m - hi.astype(np.float64)).astype(BF16)
        return hi, lo

    w1h, w1l = parts(w1)
    w1f = np.concatenate([w1h, w1l, w1h], axis=1)
    w1i = np.concatenate([w1h.T, w1l.T, w1h.T], axis=1)
    w2h, w2l = parts(w2)
    w2f = np.stack([w2h, w2l])
    w2i = np.stack([w2h.T, w2l.T])
    return w1f, w1i, tw.astype(np.float32), w2f, w2i


def round13(x):
    c = x * 2049.0
    return c - (c - x)


def pack(a, b, c, log_scale, log_shift):
    code = jnp.round(jnp.log(jnp.abs(c)) * (log_scale / LN2) + log_shift * log_scale)
    code = jnp.clip(code, 0.0, CODE_MAX)
    code = jnp.where(c < 0, -code, code)
    high = jnp.round(code * (1.0 / DIGITS))
    low = code - high * DIGITS

    def word(v, digit):
        v = jnp.where(jnp.abs(v) < TINY, TINY, round13(v))
        return v + v * (digit * STEP)

    return word(a, high), word(b, low)


def unpack(wa, wb, log_scale, log_shift):
    def parts(w):
        v = round13(w)
        digit = jnp.round((w - v) * pl.reciprocal(v * STEP, approx=True))
        return jnp.where(jnp.abs(v) <= TINY, 0.0, v), digit

    a, high = parts(wa)
    b, low = parts(wb)
    code = high * DIGITS + low
    c = jnp.exp2(jnp.abs(code) * (1.0 / log_scale) - log_shift)
    c = jnp.where(code < 0, -c, c)
    return a, b, jnp.where(code == 0, 0.0, c)


def dot(a, b):
    return jnp.dot(a, b, preferred_element_type=F32)


def dot3(x, w_ref):
    hi, lo = split(x)
    wh = w_ref[0]
    return dot(hi, wh) + (dot(hi, w_ref[1]) + dot(lo, wh))


def place(me):
    return lax.div(me, 16), lax.rem(lax.div(me, 2), 8), lax.rem(me, 2)


def peer(me, i):
    x, z, y = place(me)
    k, j = lax.div(i, 8), lax.rem(i, 8)
    dy = 1 - lax.div(k, 4)
    k = lax.rem(k, 4)
    dx = 2 + lax.div(k + 1, 2) * (1 - 2 * lax.rem(k, 2))
    dz = 4 + lax.div(j + 1, 2) * (1 - 2 * lax.rem(j, 2))
    return lax.rem(x + dx, 4) * 16 + lax.rem(z + dz, 8) * 2 + lax.rem(y + dy, 2)


def conv_kernel(
    outer_h, inner_h, value_h, cot_h, filt_h, w1f_h, w1i_h, tw_h, w2f_h, w2i_h,
    back0, back1,
    outer, inner, value, cot, filt, w1f, w1i, tw, w2f, w2i,
    send0, send1, recv0, recv1, ret0, ret1, spec, lags, part, sums,
    load_sem, send_sem, recv_sem, sendr_sem, recvr_sem, sq_send, sq_recv,
):
    me = lax.axis_index("ctx")
    ch = lax.axis_index("ch")

    loads = [
        pltpu.make_async_copy(src, dst, load_sem.at[n])
        for n, (src, dst) in enumerate(
            [
                (inner_h, inner), (value_h, value), (cot_h, cot), (outer_h, outer),
                (filt_h, filt), (w1f_h, w1f), (w1i_h, w1i), (tw_h, tw), (w2f_h, w2f),
                (w2i_h, w2i),
            ]
        )
    ]
    for load in loads:
        load.start()

    barrier = pltpu.get_barrier_semaphore()

    def greet(i, _):
        pl.semaphore_signal(
            barrier, inc=1, device_id={"ctx": peer(me, i)}, device_id_type=MESH
        )
        return 0

    lax.fori_loop(0, NCTX - 1, greet, 0)
    for j in range(1, NCH):
        pl.semaphore_signal(
            barrier, inc=1, device_id={"ch": lax.rem(ch + j, NCH)}, device_id_type=MESH
        )

    for load in loads[:5]:
        load.wait()
    mixed = inner[...].astype(F32) * value[...].astype(F32)
    gconv = cot[...].astype(F32) * outer[...].astype(F32)
    wa, wb = pack(mixed, gconv, filt[...], *FILTER_CODE)
    wa = wa.T.reshape(NCTX, NAR, BLK)
    wb = wb.T.reshape(NCTX, NAR, BLK)
    send0[...] = jnp.concatenate([wa[:, :HALF], wb[:, :HALF]], axis=1)
    send1[...] = jnp.concatenate([wa[:, HALF:], wb[:, HALF:]], axis=1)
    for load in loads[5:]:
        load.wait()

    pl.semaphore_wait(barrier, NCTX - 1 + NCH - 1)

    def spread(src, dst, send_s, recv_s):
        def one(i, _):
            to = peer(me, i)
            pltpu.make_async_remote_copy(
                src_ref=src(to),
                dst_ref=dst(me),
                send_sem=send_s,
                recv_sem=recv_s,
                device_id={"ctx": to},
                device_id_type=MESH,
            ).start()
            return 0

        lax.fori_loop(0, NCTX - 1, one, 0)
        pltpu.make_async_copy(src(me), dst(me), recv_s).start()

    def out_to(n):
        recv = (recv0, recv1)[n]
        send = (send0, send1)[n]
        spread(
            lambda d: send.at[d], lambda d: recv.at[pl.ds(d * 8, 8)],
            send_sem.at[n], recv_sem.at[n],
        )

    out_to(0)
    out_to(1)

    tr, ti = tw[0], tw[1]
    wa, wb = w1f[...], w1i[...]

    def forward(rows):
        hi, lo = split(rows)
        z = dot(wa, jnp.concatenate([hi, hi, lo], axis=0))
        zr, zi = z[:NCTX], z[NCTX:]
        return jnp.concatenate([zr * tr - zi * ti, zr * ti + zi * tr], axis=1)

    def inverse(v):
        vr, vi = v[:, :BLK], v[:, BLK:]
        u = jnp.concatenate([vr * tr + vi * ti, vi * tr - vr * ti], axis=0)
        hi, lo = split(u)
        return dot(wb, jnp.concatenate([hi, hi, lo], axis=0)) * (1.0 / (NCTX * BLK))

    def correlate(a, b):
        ar, ai, br, bi = a[:, :BLK], a[:, BLK:], b[:, :BLK], b[:, BLK:]
        return jnp.concatenate([ar * br + ai * bi, ar * bi - ai * br], axis=1)

    def convolve(a, b):
        ar, ai, br, bi = a[:, :BLK], a[:, BLK:], b[:, :BLK], b[:, BLK:]
        return jnp.concatenate([ar * br - ai * bi, ar * bi + ai * br], axis=1)

    def pieces(v):
        return [v[n * NCTX : (n + 1) * NCTX] for n in range(v.shape[0] // NCTX)]

    def taken(recv, c):
        return unpack(
            recv[pl.ds(c, NCTX, stride=8), :],
            recv[pl.ds(HALF + c, NCTX, stride=8), :],
            *FILTER_CODE,
        )

    def lag_pair(recv):
        def run(n, acc):
            c = 2 * n
            a, b = taken(recv, c), taken(recv, c + 1)
            u = [forward(v) for v in (a[0], b[0], a[1], b[1], a[2], b[2])]
            f = dot3(jnp.concatenate(u, axis=0), w2f)
            spec[n] = f
            m0, m1, g0, g1, _, _ = pieces(f)
            v = dot3(jnp.concatenate([correlate(m0, g0), correlate(m1, g1)], axis=0), w2i)
            for d, part_v in enumerate(pieces(v)):
                lag = inverse(part_v)
                lags[c + d] = lag
                acc = acc + jnp.sum((lag * lag).reshape(NCTX // 8, 8, BLK), axis=0)
            return acc

        return run

    def conv_pair(ret, stride):
        def run(n, carry):
            c = 2 * n
            m0, m1, g0, g1, f0, f1 = pieces(spec[n])
            v = dot3(
                jnp.concatenate(
                    [convolve(f0, m0), convolve(f1, m1), correlate(f0, g0), correlate(f1, g1)],
                    axis=0,
                ),
                w2i,
            )
            y0, y1, b0, b1 = [inverse(p) for p in pieces(v)]
            for d, (y, b) in enumerate([(y0, b0), (y1, b1)]):
                wa, wb = pack(y, b, lags[c + d], *LAG_CODE)
                ret[pl.ds(c + d, NCTX, stride=stride), :] = wa
                ret[pl.ds(HALF + c + d, NCTX, stride=stride), :] = wb
            return carry

        return run

    pltpu.make_async_copy(recv0, recv0, recv_sem.at[0]).wait()
    acc = lax.fori_loop(0, HALF // 2, lag_pair(recv0), jnp.zeros((8, BLK), F32))
    lax.fori_loop(0, HALF // 2, conv_pair(ret0, 8), 0)
    spread(
        lambda d: ret0.at[pl.ds(d * 8, 8)], lambda d: back0.at[d],
        sendr_sem.at[0], recvr_sem.at[0],
    )

    pltpu.make_async_copy(recv1, recv1, recv_sem.at[1]).wait()
    acc = lax.fori_loop(0, HALF // 2, lag_pair(recv1), acc)

    part[...] = acc
    sums[ch] = acc
    for j in range(1, NCH):
        pltpu.make_async_remote_copy(
            src_ref=part,
            dst_ref=sums.at[ch],
            send_sem=sq_send,
            recv_sem=sq_recv,
            device_id={"ch": lax.rem(ch + j, NCH)},
            device_id_type=MESH,
        ).start()
    lax.fori_loop(0, HALF // 2, conv_pair(ret1, 16), 0)
    seven = sums.at[pl.ds(0, NCH - 1)]
    pltpu.make_async_copy(seven, seven, sq_send).wait()
    pltpu.make_async_copy(seven, seven, sq_recv).wait()
    group = jnp.sum(jnp.sum(sums[...], axis=0), axis=0, keepdims=True)
    ret1[pl.ds(8, NCTX, stride=16), :] = jnp.broadcast_to(group, (NCTX, BLK))
    spread(
        lambda d: ret1.at[pl.ds(d * 16, 9)], lambda d: back1.at[d, pl.ds(0, 9)],
        sendr_sem.at[1], recvr_sem.at[1],
    )

    others = pl.ds(0, NCTX - 1)
    for n, ref in enumerate((send0, send1)):
        pltpu.make_async_copy(ref.at[others], ref.at[others], send_sem.at[n]).wait()
    pltpu.make_async_copy(back0.at[others], back0.at[others], sendr_sem.at[0]).wait()
    nine = back1.at[others, pl.ds(0, 9)]
    pltpu.make_async_copy(nine, nine, sendr_sem.at[1]).wait()
    pltpu.make_async_copy(back0, back0, recvr_sem.at[0]).wait()
    nine = back1.at[:, pl.ds(0, 9)]
    pltpu.make_async_copy(nine, nine, recvr_sem.at[1]).wait()


def gate_kernel(
    outer_h, inner_h, value_h, cot_h, skip, back0_h, back1_h,
    hyena, gouter, ginner, gvalue, gfilter,
    outer, inner, value, cot, back0, back1, sem,
):
    loads = [
        pltpu.make_async_copy(src, dst, sem.at[n])
        for n, (src, dst) in enumerate(
            [
                (back0_h, back0), (back1_h, back1), (inner_h, inner), (value_h, value), (outer_h, outer),
                (cot_h, cot),
            ]
        )
    ]
    for load in loads:
        load.start()
    for load in loads:
        load.wait()
    inner_f = inner[...].astype(F32)
    value_f = value[...].astype(F32)
    outer_f = outer[...].astype(F32)
    cot_f = cot[...].astype(F32)
    gain = skip[...]
    b0, b1 = back0[...], back1[...]
    wa = jnp.concatenate([b0[:, :HALF], b1[:, :HALF]], axis=1).reshape(LANES, BLK).T
    wb = jnp.concatenate([b0[:, HALF:], b1[:, HALF : 2 * HALF]], axis=1).reshape(LANES, BLK).T
    conv, corr, lag = unpack(wa, wb, *LAG_CODE)
    base = conv + gain * (inner_f * value_f)
    hyena[...] = (outer_f * base).astype(BF16)
    gouter[...] = (cot_f * base).astype(BF16)
    gmixed = corr + gain * (cot_f * outer_f)
    ginner[...] = (gmixed * value_f).astype(BF16)
    gvalue[...] = (gmixed * inner_f).astype(BF16)
    squares = jnp.sum(jnp.sum(b1[:, 8, :], axis=0, keepdims=True), axis=1, keepdims=True)
    limit = float(NCTX * BLK) * float(np.sqrt(LANES * NCH))
    scale = jnp.minimum(1.0, limit / jnp.sqrt(squares + 1e-06))
    gfilter[...] = lag * scale


def local(outer_gate, inner_gate, value_path, long_filter, skip_gain, cotangent):
    vmem = pl.BlockSpec(memory_space=pltpu.VMEM)
    hbm = pl.BlockSpec(memory_space=pltpu.HBM)
    consts = tables()
    dma = pltpu.SemaphoreType.DMA
    back0, back1 = pl.pallas_call(
        conv_kernel,
        out_shape=(
            jax.ShapeDtypeStruct((NCTX, 8, BLK), F32),
            jax.ShapeDtypeStruct((NCTX, 16, BLK), F32),
        ),
        in_specs=[hbm] * 10,
        out_specs=(hbm, hbm),
        scratch_shapes=[pltpu.VMEM((BLK, LANES), BF16)] * 4
        + [pltpu.VMEM((BLK, LANES), F32)]
        + [pltpu.VMEM(c.shape, c.dtype) for c in consts]
        + [
            pltpu.VMEM((NCTX, 8, BLK), F32),
            pltpu.VMEM((NCTX, 8, BLK), F32),
            pltpu.VMEM((NCTX * 8, BLK), F32),
            pltpu.VMEM((NCTX * 8, BLK), F32),
            pltpu.VMEM((NCTX * 8, BLK), F32),
            pltpu.VMEM((NCTX * 16, BLK), F32),
            pltpu.VMEM((HALF // 2, 6 * NCTX, 2 * BLK), F32),
            pltpu.VMEM((HALF, NCTX, BLK), F32),
            pltpu.VMEM((8, BLK), F32),
            pltpu.VMEM((NCH, 8, BLK), F32),
            dma((10,)),
        ]
        + [dma((2,))] * 4
        + [dma, dma],
        compiler_params=pltpu.CompilerParams(
            collective_id=0, has_side_effects=True, vmem_limit_bytes=VMEM_LIMIT
        ),
    )(outer_gate, inner_gate, value_path, cotangent, long_filter, *consts)
    arr = jax.ShapeDtypeStruct((BLK, LANES), BF16)
    return pl.pallas_call(
        gate_kernel,
        out_shape=(arr, arr, arr, arr, jax.ShapeDtypeStruct((BLK, LANES), F32)),
        in_specs=[hbm] * 4 + [vmem, hbm, hbm],
        out_specs=(vmem,) * 5,
        scratch_shapes=[pltpu.VMEM((BLK, LANES), BF16)] * 4
        + [
            pltpu.VMEM((NCTX, 8, BLK), F32),
            pltpu.VMEM((NCTX, 16, BLK), F32),
            dma((6,)),
        ],
        compiler_params=pltpu.CompilerParams(vmem_limit_bytes=VMEM_LIMIT),
    )(
        outer_gate, inner_gate, value_path, cotangent, skip_gain.reshape(1, LANES),
        back0, back1,
    )


def solution(mesh):
    big = P("ctx", "ch")
    return jax.shard_map(
        local,
        mesh=mesh,
        in_specs=(big, big, big, big, P("ch"), big),
        out_specs=(big,) * 5,
        check_vma=False,
    )
```

```python
import jax
import jax.numpy as jnp
import numpy as np
from jax import lax
from jax.experimental import pallas as pl
from jax.experimental.pallas import tpu as pltpu
from jax.sharding import PartitionSpec as P

F32 = jnp.float32
BF16 = jnp.bfloat16
MESH = pl.DeviceIdType.MESH

NCTX = 64
NCH = 8
VMEM_LIMIT = 60 * 1024 * 1024
BLK = 128
LANES = 512
NAR = LANES // NCTX
HALF = NAR // 2
LN2 = float(np.log(2.0))
DIGITS = 511.0
CODE_MAX = 255.0 * DIGITS + 255.0
STEP = 2.0**-22
TINY = 2.0**-80
FILTER_CODE = (CODE_MAX / 24.0, 28.0)
LAG_CODE = (CODE_MAX / 128.0, 102.0)


def split(x):
    hi = x.astype(BF16)
    lo = (x - hi.astype(F32)).astype(BF16)
    return hi, lo


def tables():
    total = NCTX * BLK
    p = np.arange(NCTX)
    s = np.arange(BLK)
    k = np.arange(NCTX) + 0.25
    a1 = 2 * np.pi * np.outer(k, p) / NCTX
    w1 = np.concatenate([np.cos(a1), -np.sin(a1)], axis=0)
    at = 2 * np.pi * np.outer(k, s) / total
    tw = np.stack([np.cos(at), -np.sin(at)])
    a2 = 2 * np.pi * (np.outer(s, s) % BLK) / BLK
    c, sn = np.cos(a2), np.sin(a2)
    w2 = np.block([[c, -sn], [sn, c]])

    def parts(m):
        hi = m.astype(BF16)
        lo = (m - hi.astype(np.float64)).astype(BF16)
        return hi, lo

    w1h, w1l = parts(w1)
    w1f = np.concatenate([w1h, w1l, w1h], axis=1)
    w1i = np.concatenate([w1h.T, w1l.T, w1h.T], axis=1)
    w2h, w2l = parts(w2)
    w2f = np.stack([w2h, w2l])
    w2i = np.stack([w2h.T, w2l.T])
    return w1f, w1i, tw.astype(np.float32), w2f, w2i


def round13(x):
    c = x * 2049.0
    return c - (c - x)


def pack(a, b, c, log_scale, log_shift):
    code = jnp.round(jnp.log(jnp.abs(c)) * (log_scale / LN2) + log_shift * log_scale)
    code = jnp.clip(code, 0.0, CODE_MAX)
    code = jnp.where(c < 0, -code, code)
    high = jnp.round(code * (1.0 / DIGITS))
    low = code - high * DIGITS

    def word(v, digit):
        v = jnp.where(jnp.abs(v) < TINY, TINY, round13(v))
        return v + v * (digit * STEP)

    return word(a, high), word(b, low)


def unpack(wa, wb, log_scale, log_shift):
    def parts(w):
        v = round13(w)
        digit = jnp.round((w - v) * pl.reciprocal(v * STEP, approx=True))
        return jnp.where(jnp.abs(v) <= TINY, 0.0, v), digit

    a, high = parts(wa)
    b, low = parts(wb)
    code = high * DIGITS + low
    c = jnp.exp2(jnp.abs(code) * (1.0 / log_scale) - log_shift)
    c = jnp.where(code < 0, -c, c)
    return a, b, jnp.where(code == 0, 0.0, c)


def dot(a, b):
    return jnp.dot(a, b, preferred_element_type=F32)


def dot3(x, w_ref):
    hi, lo = split(x)
    wh = w_ref[0]
    return dot(hi, wh) + (dot(hi, w_ref[1]) + dot(lo, wh))


def place(me):
    return lax.div(me, 16), lax.rem(lax.div(me, 2), 8), lax.rem(me, 2)


def peer(me, i):
    x, z, y = place(me)
    k, j = lax.div(i, 8), lax.rem(i, 8)
    dy = 1 - lax.div(k, 4)
    k = lax.rem(k, 4)
    dx = 2 + lax.div(k + 1, 2) * (1 - 2 * lax.rem(k, 2))
    dz = 4 + lax.div(j + 1, 2) * (1 - 2 * lax.rem(j, 2))
    return lax.rem(x + dx, 4) * 16 + lax.rem(z + dz, 8) * 2 + lax.rem(y + dy, 2)


def ranked(me, i):
    x, z, y = place(me)
    g, r = lax.div(i, 16), lax.rem(i, 16)
    dy = 1 - lax.div(r, 8)
    r = lax.rem(r, 8)
    k, j = lax.div(r, 2), lax.rem(r, 2)
    dx = 2 + lax.div(k + 1, 2) * (1 - 2 * lax.rem(k, 2))
    low = lax.rem(z + j, 2)
    return lax.rem(x + dx, 4) * 16 + (2 * g + low) * 2 + lax.rem(y + dy, 2)


def conv_kernel(
    outer_h, inner_h, value_h, cot_h, filt_h, w1f_h, w1i_h, tw_h, w2f_h, w2i_h,
    back0, back1,
    outer, inner, value, cot, filt, w1f, w1i, tw, w2f, w2i,
    send0, send1, recv0, recv1, ret0, ret1, spec, lags, part, sums,
    load_sem, send_sem, recv_sem, sendr_sem, recvr_sem, sq_send, sq_recv,
):
    me = lax.axis_index("ctx")
    ch = lax.axis_index("ch")

    loads = [
        pltpu.make_async_copy(src, dst, load_sem.at[n])
        for n, (src, dst) in enumerate(
            [
                (inner_h, inner), (value_h, value), (cot_h, cot), (outer_h, outer),
                (filt_h, filt), (w1f_h, w1f), (w1i_h, w1i), (tw_h, tw), (w2f_h, w2f),
                (w2i_h, w2i),
            ]
        )
    ]
    for load in loads:
        load.start()

    barrier = pltpu.get_barrier_semaphore()

    def greet(i, _):
        pl.semaphore_signal(
            barrier, inc=1, device_id={"ctx": peer(me, i)}, device_id_type=MESH
        )
        return 0

    lax.fori_loop(0, NCTX - 1, greet, 0, unroll=7)
    for j in range(1, NCH):
        pl.semaphore_signal(
            barrier, inc=1, device_id={"ch": lax.rem(ch + j, NCH)}, device_id_type=MESH
        )

    for load in loads[:5]:
        load.wait()
    mixed = inner[...].astype(F32) * value[...].astype(F32)
    gconv = cot[...].astype(F32) * outer[...].astype(F32)
    wa, wb = pack(mixed, gconv, filt[...], *FILTER_CODE)
    wa = wa.T.reshape(NCTX, NAR, BLK)
    wb = wb.T.reshape(NCTX, NAR, BLK)
    send0[...] = jnp.concatenate([wa[:, :HALF], wb[:, :HALF]], axis=1)
    send1[...] = jnp.concatenate([wa[:, HALF:], wb[:, HALF:]], axis=1)
    for load in loads[5:]:
        load.wait()

    pl.semaphore_wait(barrier, NCTX - 1 + NCH - 1)

    def spread(src, dst, send_s, recv_s):
        def one(i, _):
            to = peer(me, i)
            pltpu.make_async_remote_copy(
                src_ref=src(to),
                dst_ref=dst(me),
                send_sem=send_s,
                recv_sem=recv_s,
                device_id={"ctx": to},
                device_id_type=MESH,
            ).start()
            return 0

        lax.fori_loop(0, NCTX - 1, one, 0, unroll=7)
        pltpu.make_async_copy(src(me), dst(me), recv_s).start()

    def spread_ranked(src, dst, send_s, recv_s, first, last):
        def one(i, _):
            to = ranked(me, i)

            @pl.when(to != me)
            def _():
                pltpu.make_async_remote_copy(
                    src_ref=src(to),
                    dst_ref=dst(me),
                    send_sem=send_s,
                    recv_sem=recv_s,
                    device_id={"ctx": to},
                    device_id_type=MESH,
                ).start()

            return 0

        lax.fori_loop(first, last, one, 0, unroll=4)
        if first == 0:
            pltpu.make_async_copy(src(me), dst(me), recv_s).start()

    def out_to(n):
        recv = (recv0, recv1)[n]
        send = (send0, send1)[n]
        spread(
            lambda d: send.at[d], lambda d: recv.at[pl.ds(d * 8, 8)],
            send_sem.at[n], recv_sem.at[n],
        )

    out_to(0)
    out_to(1)

    tr, ti = tw[0], tw[1]
    wa, wb = w1f[...], w1i[...]

    def forward(rows):
        hi, lo = split(rows)
        z = dot(wa, jnp.concatenate([hi, hi, lo], axis=0))
        zr, zi = z[:NCTX], z[NCTX:]
        return jnp.concatenate([zr * tr - zi * ti, zr * ti + zi * tr], axis=1)

    def inverse(v):
        vr, vi = v[:, :BLK], v[:, BLK:]
        u = jnp.concatenate([vr * tr + vi * ti, vi * tr - vr * ti], axis=0)
        hi, lo = split(u)
        return dot(wb, jnp.concatenate([hi, hi, lo], axis=0)) * (1.0 / (NCTX * BLK))

    def correlate(a, b):
        ar, ai, br, bi = a[:, :BLK], a[:, BLK:], b[:, :BLK], b[:, BLK:]
        return jnp.concatenate([ar * br + ai * bi, ar * bi - ai * br], axis=1)

    def convolve(a, b):
        ar, ai, br, bi = a[:, :BLK], a[:, BLK:], b[:, :BLK], b[:, BLK:]
        return jnp.concatenate([ar * br - ai * bi, ar * bi + ai * br], axis=1)

    def pieces(v):
        return [v[n * NCTX : (n + 1) * NCTX] for n in range(v.shape[0] // NCTX)]

    def taken(recv, c):
        return unpack(
            recv[pl.ds(c, NCTX, stride=8), :],
            recv[pl.ds(HALF + c, NCTX, stride=8), :],
            *FILTER_CODE,
        )

    def lag_pair(recv):
        def run(n, acc):
            c = 2 * n
            a, b = taken(recv, c), taken(recv, c + 1)
            u = [forward(v) for v in (a[0], b[0], a[1], b[1], a[2], b[2])]
            f = dot3(jnp.concatenate(u, axis=0), w2f)
            spec[n] = f
            m0, m1, g0, g1, _, _ = pieces(f)
            v = dot3(jnp.concatenate([correlate(m0, g0), correlate(m1, g1)], axis=0), w2i)
            for d, part_v in enumerate(pieces(v)):
                lag = inverse(part_v)
                lags[c + d] = lag
                acc = acc + jnp.sum((lag * lag).reshape(NCTX // 8, 8, BLK), axis=0)
            return acc

        return run

    def conv_pair(ret, stride):
        def run(n, carry):
            c = 2 * n
            m0, m1, g0, g1, f0, f1 = pieces(spec[n])
            v = dot3(
                jnp.concatenate(
                    [convolve(f0, m0), convolve(f1, m1), correlate(f0, g0), correlate(f1, g1)],
                    axis=0,
                ),
                w2i,
            )
            y0, y1, b0, b1 = [inverse(p) for p in pieces(v)]
            for d, (y, b) in enumerate([(y0, b0), (y1, b1)]):
                wa, wb = pack(y, b, lags[c + d], *LAG_CODE)
                ret[pl.ds(c + d, NCTX, stride=stride), :] = wa
                ret[pl.ds(HALF + c + d, NCTX, stride=stride), :] = wb
            return carry

        return run

    pltpu.make_async_copy(recv0, recv0, recv_sem.at[0]).wait()
    acc = lax.fori_loop(0, HALF // 2, lag_pair(recv0), jnp.zeros((8, BLK), F32))
    lax.fori_loop(0, HALF // 2, conv_pair(ret0, 8), 0)
    spread_ranked(
        lambda d: ret0.at[pl.ds(d * 8, 8)], lambda d: back0.at[d],
        sendr_sem.at[0], recvr_sem.at[0], 0, 64
    )

    pltpu.make_async_copy(recv1, recv1, recv_sem.at[1]).wait()
    acc = lax.fori_loop(0, HALF // 2, lag_pair(recv1), acc)

    part[...] = acc
    sums[ch] = acc
    for j in range(1, NCH):
        pltpu.make_async_remote_copy(
            src_ref=part,
            dst_ref=sums.at[ch],
            send_sem=sq_send,
            recv_sem=sq_recv,
            device_id={"ch": lax.rem(ch + j, NCH)},
            device_id_type=MESH,
        ).start()
    lax.fori_loop(0, HALF // 2, conv_pair(ret1, 16), 0)
    seven = sums.at[pl.ds(0, NCH - 1)]
    pltpu.make_async_copy(seven, seven, sq_send).wait()
    pltpu.make_async_copy(seven, seven, sq_recv).wait()
    group = jnp.sum(jnp.sum(sums[...], axis=0), axis=0, keepdims=True)
    ret1[pl.ds(8, NCTX, stride=16), :] = jnp.broadcast_to(group, (NCTX, BLK))
    spread_ranked(
        lambda d: ret1.at[pl.ds(d * 16, 9)], lambda d: back1.at[d, pl.ds(0, 9)],
        sendr_sem.at[1], recvr_sem.at[1], 0, 64,
    )

    others = pl.ds(0, NCTX - 1)
    for n, ref in enumerate((send0, send1)):
        pltpu.make_async_copy(ref.at[others], ref.at[others], send_sem.at[n]).wait()
    pltpu.make_async_copy(back0.at[others], back0.at[others], sendr_sem.at[0]).wait()
    nine = back1.at[others, pl.ds(0, 9)]
    pltpu.make_async_copy(nine, nine, sendr_sem.at[1]).wait()
    pltpu.make_async_copy(back0, back0, recvr_sem.at[0]).wait()
    nine = back1.at[:, pl.ds(0, 9)]
    pltpu.make_async_copy(nine, nine, recvr_sem.at[1]).wait()


def gate_kernel(
    outer_h, inner_h, value_h, cot_h, skip_h, back0_h, back1_h,
    hyena, gouter, ginner, gvalue, gfilter,
    outer, inner, value, cot, back0, back1, skip, sem,
):
    loads = [
        pltpu.make_async_copy(src, dst, sem.at[n])
        for n, (src, dst) in enumerate(
            [
                (back0_h, back0), (back1_h, back1), (inner_h, inner), (value_h, value), (outer_h, outer),
                (cot_h, cot), (skip_h, skip),
            ]
        )
    ]
    for load in loads:
        load.start()
    for load in loads:
        load.wait()
    inner_f = inner[...].astype(F32)
    value_f = value[...].astype(F32)
    outer_f = outer[...].astype(F32)
    cot_f = cot[...].astype(F32)
    gain = skip[...]
    b0, b1 = back0[...], back1[...]
    wa = jnp.concatenate([b0[:, :HALF], b1[:, :HALF]], axis=1).reshape(LANES, BLK).T
    wb = jnp.concatenate([b0[:, HALF:], b1[:, HALF : 2 * HALF]], axis=1).reshape(LANES, BLK).T
    conv, corr, lag = unpack(wa, wb, *LAG_CODE)
    base = conv + gain * (inner_f * value_f)
    hyena[...] = (outer_f * base).astype(BF16)
    gouter[...] = (cot_f * base).astype(BF16)
    gmixed = corr + gain * (cot_f * outer_f)
    ginner[...] = (gmixed * value_f).astype(BF16)
    gvalue[...] = (gmixed * inner_f).astype(BF16)
    squares = jnp.sum(jnp.sum(b1[:, 8, :], axis=0, keepdims=True), axis=1, keepdims=True)
    limit = float(NCTX * BLK) * float(np.sqrt(LANES * NCH))
    scale = jnp.minimum(1.0, limit / jnp.sqrt(squares + 1e-06))
    gfilter[...] = lag * scale


def local(outer_gate, inner_gate, value_path, long_filter, skip_gain, cotangent):
    vmem = pl.BlockSpec(memory_space=pltpu.VMEM)
    hbm = pl.BlockSpec(memory_space=pltpu.HBM)
    consts = tables()
    dma = pltpu.SemaphoreType.DMA
    back0, back1 = pl.pallas_call(
        conv_kernel,
        out_shape=(
            jax.ShapeDtypeStruct((NCTX, 8, BLK), F32),
            jax.ShapeDtypeStruct((NCTX, 16, BLK), F32),
        ),
        in_specs=[hbm] * 10,
        out_specs=(hbm, hbm),
        scratch_shapes=[pltpu.VMEM((BLK, LANES), BF16)] * 4
        + [pltpu.VMEM((BLK, LANES), F32)]
        + [pltpu.VMEM(c.shape, c.dtype) for c in consts]
        + [
            pltpu.VMEM((NCTX, 8, BLK), F32),
            pltpu.VMEM((NCTX, 8, BLK), F32),
            pltpu.VMEM((NCTX * 8, BLK), F32),
            pltpu.VMEM((NCTX * 8, BLK), F32),
            pltpu.VMEM((NCTX * 8, BLK), F32),
            pltpu.VMEM((NCTX * 16, BLK), F32),
            pltpu.VMEM((HALF // 2, 6 * NCTX, 2 * BLK), F32),
            pltpu.VMEM((HALF, NCTX, BLK), F32),
            pltpu.VMEM((8, BLK), F32),
            pltpu.VMEM((NCH, 8, BLK), F32),
            dma((10,)),
        ]
        + [dma((2,))] * 4
        + [dma, dma],
        compiler_params=pltpu.CompilerParams(
            collective_id=0, has_side_effects=True, vmem_limit_bytes=VMEM_LIMIT
        ),
    )(outer_gate, inner_gate, value_path, cotangent, long_filter, *consts)
    arr = jax.ShapeDtypeStruct((BLK, LANES), BF16)
    return pl.pallas_call(
        gate_kernel,
        out_shape=(arr, arr, arr, arr, jax.ShapeDtypeStruct((BLK, LANES), F32)),
        in_specs=[hbm] * 7,
        out_specs=(vmem,) * 5,
        scratch_shapes=[pltpu.VMEM((BLK, LANES), BF16)] * 4
        + [
            pltpu.VMEM((NCTX, 8, BLK), F32),
            pltpu.VMEM((NCTX, 16, BLK), F32),
            pltpu.VMEM((1, LANES), F32),
            dma((7,)),
        ],
        compiler_params=pltpu.CompilerParams(vmem_limit_bytes=VMEM_LIMIT),
    )(
        outer_gate, inner_gate, value_path, cotangent, skip_gain.reshape(1, LANES),
        back0, back1,
    )


def solution(mesh):
    big = P("ctx", "ch")
    return jax.shard_map(
        local,
        mesh=mesh,
        in_specs=(big, big, big, big, P("ch"), big),
        out_specs=(big,) * 5,
        check_vma=False,
    )
```

```python
import jax
import jax.numpy as jnp
import numpy as np
from jax import lax
from jax.experimental import pallas as pl
from jax.experimental.pallas import tpu as pltpu
from jax.sharding import PartitionSpec as P

F32 = jnp.float32
BF16 = jnp.bfloat16
MESH = pl.DeviceIdType.MESH

NCTX = 64
NCH = 8
VMEM_LIMIT = 60 * 1024 * 1024
BLK = 128
LANES = 512
NAR = LANES // NCTX
HALF = NAR // 2
LN2 = float(np.log(2.0))
DIGITS = 511.0
CODE_MAX = 255.0 * DIGITS + 255.0
STEP = 2.0**-22
TINY = 2.0**-80
FILTER_CODE = (CODE_MAX / 24.0, 28.0)
LAG_CODE = (CODE_MAX / 128.0, 102.0)


def split(x):
    hi = x.astype(BF16)
    lo = (x - hi.astype(F32)).astype(BF16)
    return hi, lo


def tables():
    total = NCTX * BLK
    p = np.arange(NCTX)
    s = np.arange(BLK)
    k = np.arange(NCTX) + 0.25
    a1 = 2 * np.pi * np.outer(k, p) / NCTX
    w1 = np.concatenate([np.cos(a1), -np.sin(a1)], axis=0)
    at = 2 * np.pi * np.outer(k, s) / total
    tw = np.stack([np.cos(at), -np.sin(at)])
    a2 = 2 * np.pi * (np.outer(s, s) % BLK) / BLK
    c, sn = np.cos(a2), np.sin(a2)
    w2 = np.block([[c, -sn], [sn, c]])

    def parts(m):
        hi = m.astype(BF16)
        lo = (m - hi.astype(np.float64)).astype(BF16)
        return hi, lo

    w1h, w1l = parts(w1)
    w1f = np.concatenate([w1h, w1l, w1h], axis=1)
    w1i = np.concatenate([w1h.T, w1l.T, w1h.T], axis=1)
    w2h, w2l = parts(w2)
    w2f = np.stack([w2h, w2l])
    w2i = np.stack([w2h.T, w2l.T])
    return w1f, w1i, tw.astype(np.float32), w2f, w2i


def round13(x):
    c = x * 2049.0
    return c - (c - x)


def pack(a, b, c, log_scale, log_shift):
    code = jnp.round(jnp.log(jnp.abs(c)) * (log_scale / LN2) + log_shift * log_scale)
    code = jnp.clip(code, 0.0, CODE_MAX)
    code = jnp.where(c < 0, -code, code)
    high = jnp.round(code * (1.0 / DIGITS))
    low = code - high * DIGITS

    def word(v, digit):
        v = jnp.where(jnp.abs(v) < TINY, TINY, round13(v))
        return v + v * (digit * STEP)

    return word(a, high), word(b, low)


def unpack(wa, wb, log_scale, log_shift):
    def parts(w):
        v = round13(w)
        digit = jnp.round((w - v) * pl.reciprocal(v * STEP, approx=True))
        return jnp.where(jnp.abs(v) <= TINY, 0.0, v), digit

    a, high = parts(wa)
    b, low = parts(wb)
    code = high * DIGITS + low
    c = jnp.exp2(jnp.abs(code) * (1.0 / log_scale) - log_shift)
    c = jnp.where(code < 0, -c, c)
    return a, b, jnp.where(code == 0, 0.0, c)


def dot(a, b):
    return jnp.dot(a, b, preferred_element_type=F32)


def dot3(x, w_ref):
    hi, lo = split(x)
    wh = w_ref[0]
    return dot(hi, wh) + (dot(hi, w_ref[1]) + dot(lo, wh))


def place(me):
    return lax.div(me, 16), lax.rem(lax.div(me, 2), 8), lax.rem(me, 2)


def peer(me, i):
    x, z, y = place(me)
    k, j = lax.div(i, 8), lax.rem(i, 8)
    dy = 1 - lax.div(k, 4)
    k = lax.rem(k, 4)
    dx = 2 + lax.div(k + 1, 2) * (1 - 2 * lax.rem(k, 2))
    dz = 4 + lax.div(j + 1, 2) * (1 - 2 * lax.rem(j, 2))
    return lax.rem(x + dx, 4) * 16 + lax.rem(z + dz, 8) * 2 + lax.rem(y + dy, 2)


def ranked(me, i):
    x, z, y = place(me)
    g, r = lax.div(i, 16), lax.rem(i, 16)
    dy = 1 - lax.rem(r, 2)
    r = lax.div(r, 2)
    k, j = lax.div(r, 2), lax.rem(r, 2)
    dx = 2 + lax.div(k + 1, 2) * (1 - 2 * lax.rem(k, 2))
    low = lax.rem(z + j, 2)
    return lax.rem(x + dx, 4) * 16 + (2 * g + low) * 2 + lax.rem(y + dy, 2)


def conv_kernel(
    outer_h, inner_h, value_h, cot_h, filt_h, w1f_h, w1i_h, tw_h, w2f_h, w2i_h,
    back0, back1,
    outer, inner, value, cot, filt, w1f, w1i, tw, w2f, w2i,
    send0, send1, recv0, recv1, ret0, ret1, spec, lags, part, sums,
    load_sem, send_sem, recv_sem, sendr_sem, recvr_sem, sq_send, sq_recv,
):
    me = lax.axis_index("ctx")
    ch = lax.axis_index("ch")

    loads = [
        pltpu.make_async_copy(src, dst, load_sem.at[n])
        for n, (src, dst) in enumerate(
            [
                (inner_h, inner), (value_h, value), (cot_h, cot), (outer_h, outer),
                (filt_h, filt), (w1f_h, w1f), (w1i_h, w1i), (tw_h, tw), (w2f_h, w2f),
                (w2i_h, w2i),
            ]
        )
    ]
    for load in loads[:5]:
        load.start()

    barrier = pltpu.get_barrier_semaphore()

    def greet(i, _):
        pl.semaphore_signal(
            barrier, inc=1, device_id={"ctx": peer(me, i)}, device_id_type=MESH
        )
        return 0

    lax.fori_loop(0, NCTX - 1, greet, 0, unroll=7)
    for j in range(1, NCH):
        pl.semaphore_signal(
            barrier, inc=1, device_id={"ch": lax.rem(ch + j, NCH)}, device_id_type=MESH
        )

    for load in loads[5:]:
        load.start()

    for load in loads[:5]:
        load.wait()
    mixed = inner[...].astype(F32) * value[...].astype(F32)
    gconv = cot[...].astype(F32) * outer[...].astype(F32)
    wa, wb = pack(mixed, gconv, filt[...], *FILTER_CODE)
    wa = wa.T.reshape(NCTX, NAR, BLK)
    wb = wb.T.reshape(NCTX, NAR, BLK)
    send0[...] = jnp.concatenate([wa[:, :HALF], wb[:, :HALF]], axis=1)
    send1[...] = jnp.concatenate([wa[:, HALF:], wb[:, HALF:]], axis=1)
    for load in loads[5:]:
        load.wait()

    pl.semaphore_wait(barrier, NCTX - 1 + NCH - 1)

    def spread(src, dst, send_s, recv_s):
        def one(i, _):
            to = peer(me, i)
            pltpu.make_async_remote_copy(
                src_ref=src(to),
                dst_ref=dst(me),
                send_sem=send_s,
                recv_sem=recv_s,
                device_id={"ctx": to},
                device_id_type=MESH,
            ).start()
            return 0

        lax.fori_loop(0, NCTX - 1, one, 0, unroll=7)
        pltpu.make_async_copy(src(me), dst(me), recv_s).start()

    def spread_ranked(src, dst, send_s, recv_s, first, last):
        def one(i, _):
            to = ranked(me, i)

            @pl.when(to != me)
            def _():
                pltpu.make_async_remote_copy(
                    src_ref=src(to),
                    dst_ref=dst(me),
                    send_sem=send_s,
                    recv_sem=recv_s,
                    device_id={"ctx": to},
                    device_id_type=MESH,
                ).start()

            return 0

        lax.fori_loop(first, last, one, 0, unroll=4)
        if first == 0:
            pltpu.make_async_copy(src(me), dst(me), recv_s).start()

    def out_to(n):
        recv = (recv0, recv1)[n]
        send = (send0, send1)[n]
        spread(
            lambda d: send.at[d], lambda d: recv.at[pl.ds(d * 8, 8)],
            send_sem.at[n], recv_sem.at[n],
        )

    out_to(0)
    out_to(1)

    tr, ti = tw[0], tw[1]
    wa, wb = w1f[...], w1i[...]

    def forward(rows0, rows1):
        h0, l0 = split(rows0)
        h1, l1 = split(rows1)
        hi = jnp.concatenate([h0, h1], axis=1)
        lo = jnp.concatenate([l0, l1], axis=1)
        z = dot(wa, jnp.concatenate([hi, hi, lo], axis=0))
        out = []
        for d in (0, 1):
            zr, zi = z[:NCTX, d * BLK : (d + 1) * BLK], z[NCTX:, d * BLK : (d + 1) * BLK]
            out.append(jnp.concatenate([zr * tr - zi * ti, zr * ti + zi * tr], axis=1))
        return out

    def inverse(v0, v1):
        us = []
        for v in (v0, v1):
            vr, vi = v[:, :BLK], v[:, BLK:]
            us.append(jnp.concatenate([vr * tr + vi * ti, vi * tr - vr * ti], axis=0))
        hi, lo = split(jnp.concatenate(us, axis=1))
        y = dot(wb, jnp.concatenate([hi, hi, lo], axis=0)) * (1.0 / (NCTX * BLK))
        return y[:, :BLK], y[:, BLK:]

    def correlate(a, b):
        ar, ai, br, bi = a[:, :BLK], a[:, BLK:], b[:, :BLK], b[:, BLK:]
        return jnp.concatenate([ar * br + ai * bi, ar * bi - ai * br], axis=1)

    def convolve(a, b):
        ar, ai, br, bi = a[:, :BLK], a[:, BLK:], b[:, :BLK], b[:, BLK:]
        return jnp.concatenate([ar * br - ai * bi, ar * bi + ai * br], axis=1)

    def pieces(v):
        return [v[n * NCTX : (n + 1) * NCTX] for n in range(v.shape[0] // NCTX)]

    tiles = pl.ds(0, NCTX * 8)

    def taken(recv, c):
        return unpack(
            recv[pl.ds(c, NCTX, stride=8), :],
            recv[pl.ds(HALF + c, NCTX, stride=8), :],
            *FILTER_CODE,
        )

    def lag_half(recv, acc):
        us = []
        for c in range(0, HALF, 2):
            a, b = taken(recv, c), taken(recv, c + 1)
            us += forward(a[0], b[0]) + forward(a[1], b[1]) + forward(a[2], b[2])
        f = dot3(jnp.concatenate(us, axis=0), w2f)
        spec[...] = f
        f = pieces(f)
        prods = []
        for c in range(0, HALF, 2):
            m0, m1, g0, g1 = f[3 * c : 3 * c + 4]
            prods += [correlate(m0, g0), correlate(m1, g1)]
        v = pieces(dot3(jnp.concatenate(prods, axis=0), w2i))
        for c in range(0, HALF, 2):
            for d, lag in enumerate(inverse(v[c], v[c + 1])):
                lags[c + d] = lag
                acc = acc + jnp.sum((lag * lag).reshape(NCTX // 8, 8, BLK), axis=0)
        return acc

    def conv_half(ret, stride):
        f = pieces(spec[...])
        prods = []
        for c in range(0, HALF, 2):
            m0, m1, g0, g1, f0, f1 = f[3 * c : 3 * c + 6]
            prods += [convolve(f0, m0), convolve(f1, m1), correlate(f0, g0), correlate(f1, g1)]
        v = pieces(dot3(jnp.concatenate(prods, axis=0), w2i))
        for c in range(0, HALF, 2):
            ys = inverse(v[2 * c], v[2 * c + 1])
            bs = inverse(v[2 * c + 2], v[2 * c + 3])
            for d in (0, 1):
                wa, wb = pack(ys[d], bs[d], lags[c + d], *LAG_CODE)
                ret[pl.ds(c + d, NCTX, stride=stride), :] = wa
                ret[pl.ds(HALF + c + d, NCTX, stride=stride), :] = wb

    pltpu.make_async_copy(recv0.at[tiles], recv0.at[tiles], recv_sem.at[0]).wait()
    acc = lag_half(recv0, jnp.zeros((8, BLK), F32))
    conv_half(ret0, 8)
    spread_ranked(
        lambda d: ret0.at[pl.ds(d * 8, 8)], lambda d: back0.at[d],
        sendr_sem.at[0], recvr_sem.at[0], 0, 64
    )

    pltpu.make_async_copy(recv1.at[tiles], recv1.at[tiles], recv_sem.at[1]).wait()
    acc = lag_half(recv1, acc)

    part[...] = acc
    sums[ch] = acc
    for j in range(1, NCH):
        pltpu.make_async_remote_copy(
            src_ref=part,
            dst_ref=sums.at[ch],
            send_sem=sq_send,
            recv_sem=sq_recv,
            device_id={"ch": lax.rem(ch + j, NCH)},
            device_id_type=MESH,
        ).start()
    conv_half(ret1, 16)
    seven = sums.at[pl.ds(0, NCH - 1)]
    pltpu.make_async_copy(seven, seven, sq_send).wait()
    pltpu.make_async_copy(seven, seven, sq_recv).wait()
    group = jnp.sum(jnp.sum(sums[...], axis=0), axis=0, keepdims=True)
    ret1[pl.ds(8, NCTX, stride=16), :] = jnp.broadcast_to(group, (NCTX, BLK))
    spread_ranked(
        lambda d: ret1.at[pl.ds(d * 16, 9)], lambda d: back1.at[d, pl.ds(0, 9)],
        sendr_sem.at[1], recvr_sem.at[1], 0, 64,
    )

    others = pl.ds(0, NCTX - 1)
    for n, ref in enumerate((send0, send1)):
        pltpu.make_async_copy(ref.at[others], ref.at[others], send_sem.at[n]).wait()
    pltpu.make_async_copy(back0.at[others], back0.at[others], sendr_sem.at[0]).wait()
    nine = back1.at[others, pl.ds(0, 9)]
    pltpu.make_async_copy(nine, nine, sendr_sem.at[1]).wait()
    pltpu.make_async_copy(back0, back0, recvr_sem.at[0]).wait()
    nine = back1.at[:, pl.ds(0, 9)]
    pltpu.make_async_copy(nine, nine, recvr_sem.at[1]).wait()


def gate_kernel(
    outer_h, inner_h, value_h, cot_h, skip_h, back0_h, back1_h,
    hyena, gouter, ginner, gvalue, gfilter,
    outer, inner, value, cot, back0, back1, skip, sem,
):
    loads = [
        pltpu.make_async_copy(src, dst, sem.at[n])
        for n, (src, dst) in enumerate(
            [
                (back0_h, back0), (back1_h, back1), (inner_h, inner), (value_h, value), (outer_h, outer),
                (cot_h, cot), (skip_h, skip),
            ]
        )
    ]
    for load in loads:
        load.start()
    for load in loads:
        load.wait()
    inner_f = inner[...].astype(F32)
    value_f = value[...].astype(F32)
    outer_f = outer[...].astype(F32)
    cot_f = cot[...].astype(F32)
    gain = skip[...]
    b0, b1 = back0[...], back1[...]
    wa = jnp.concatenate([b0[:, :HALF], b1[:, :HALF]], axis=1).reshape(LANES, BLK).T
    wb = jnp.concatenate([b0[:, HALF:], b1[:, HALF : 2 * HALF]], axis=1).reshape(LANES, BLK).T
    conv, corr, lag = unpack(wa, wb, *LAG_CODE)
    base = conv + gain * (inner_f * value_f)
    hyena[...] = (outer_f * base).astype(BF16)
    gouter[...] = (cot_f * base).astype(BF16)
    gmixed = corr + gain * (cot_f * outer_f)
    ginner[...] = (gmixed * value_f).astype(BF16)
    gvalue[...] = (gmixed * inner_f).astype(BF16)
    squares = jnp.sum(jnp.sum(b1[:, 8, :], axis=0, keepdims=True), axis=1, keepdims=True)
    limit = float(NCTX * BLK) * float(np.sqrt(LANES * NCH))
    scale = jnp.minimum(1.0, limit / jnp.sqrt(squares + 1e-06))
    gfilter[...] = lag * scale


def local(outer_gate, inner_gate, value_path, long_filter, skip_gain, cotangent):
    vmem = pl.BlockSpec(memory_space=pltpu.VMEM)
    hbm = pl.BlockSpec(memory_space=pltpu.HBM)
    consts = tables()
    dma = pltpu.SemaphoreType.DMA
    back0, back1 = pl.pallas_call(
        conv_kernel,
        out_shape=(
            jax.ShapeDtypeStruct((NCTX, 8, BLK), F32),
            jax.ShapeDtypeStruct((NCTX, 16, BLK), F32),
        ),
        in_specs=[hbm] * 10,
        out_specs=(hbm, hbm),
        scratch_shapes=[pltpu.VMEM((BLK, LANES), BF16)] * 4
        + [pltpu.VMEM((BLK, LANES), F32)]
        + [pltpu.VMEM(c.shape, c.dtype) for c in consts]
        + [
            pltpu.VMEM((NCTX, 8, BLK), F32),
            pltpu.VMEM((NCTX, 8, BLK), F32),
            pltpu.VMEM((NCTX * 8 + 8, BLK), F32),
            pltpu.VMEM((NCTX * 8 + 8, BLK), F32),
            pltpu.VMEM((NCTX * 8 + 8, BLK), F32),
            pltpu.VMEM((NCTX * 16 + 16, BLK), F32),
            pltpu.VMEM((3 * HALF * NCTX, 2 * BLK), F32),
            pltpu.VMEM((HALF, NCTX, BLK), F32),
            pltpu.VMEM((8, BLK), F32),
            pltpu.VMEM((NCH, 8, BLK), F32),
            dma((10,)),
        ]
        + [dma((2,))] * 4
        + [dma, dma],
        compiler_params=pltpu.CompilerParams(
            collective_id=0, has_side_effects=True, vmem_limit_bytes=VMEM_LIMIT
        ),
    )(outer_gate, inner_gate, value_path, cotangent, long_filter, *consts)
    arr = jax.ShapeDtypeStruct((BLK, LANES), BF16)
    return pl.pallas_call(
        gate_kernel,
        out_shape=(arr, arr, arr, arr, jax.ShapeDtypeStruct((BLK, LANES), F32)),
        in_specs=[hbm] * 7,
        out_specs=(vmem,) * 5,
        scratch_shapes=[pltpu.VMEM((BLK, LANES), BF16)] * 4
        + [
            pltpu.VMEM((NCTX, 8, BLK), F32),
            pltpu.VMEM((NCTX, 16, BLK), F32),
            pltpu.VMEM((1, LANES), F32),
            dma((7,)),
        ],
        compiler_params=pltpu.CompilerParams(vmem_limit_bytes=VMEM_LIMIT),
    )(
        outer_gate, inner_gate, value_path, cotangent, skip_gain.reshape(1, LANES),
        back0, back1,
    )


def solution(mesh):
    big = P("ctx", "ch")
    return jax.shard_map(
        local,
        mesh=mesh,
        in_specs=(big, big, big, big, P("ch"), big),
        out_specs=(big,) * 5,
        check_vma=False,
    )
```
